32 devices in a mesh: width: 2 (over x), seqo: 4 (over y, core), seqi: 4 (over z).
Axes of the slice: x: 2, y: 2, z: 4, core: 2. Of those that a mesh axis runs over, the one named last changes fastest.
Arguments:
- rows_in: bfloat16 [4096, 2048], P(('seqo', 'seqi'), 'width'), may hold values from -6 to 6
- owner: int32 [4096, 1], P(('seqo', 'seqi')), may hold values from 0 to 15; in each aligned block of 256 rows (0 to 255, 256 to 511, ...) at most 32 rows name the same one
- first_blocks: bfloat16 [16, 512, 512], P(('seqo', 'seqi')), may hold values from -0.25 to 0.25
- middle_blocks: bfloat16 [512, 16, 16], P(('seqo', 'seqi')), may hold values from -1.5 to 1.5
- last_blocks: bfloat16 [16, 512, 512], P(('seqo', 'seqi')), may hold values from -0.25 to 0.25
- kernel: bfloat16 [16, 512, 2048], P(None, ('seqo', 'seqi'), 'width'), may hold values from -6 to 6
- gate_gain: float32 [2048], P('width'), may hold values from -4 to 4
- gate_bias: float32 [2048], P('width'), may hold values from -4 to 4
- cotangent: bfloat16 [8192, 2048], P(('seqo', 'seqi'), 'width'), may hold values from -6 to 6
Outputs:
- grad_rows: bfloat16 [4096, 2048], P(('seqo', 'seqi'), 'width')
- grad_middle: float32 [512, 16, 16], P(('seqo', 'seqi'), 'width')
- grad_last: float32 [16, 512, 512], P(('seqo', 'seqi'), 'width')
- grad_kernel: bfloat16 [16, 512, 2048], P(None, ('seqo', 'seqi'), 'width')
The draws below stay inside these ranges and needn't reach their ends.
Inputs may be any that keep to these rules, and one draw needn't show every extreme that they name: Owners are numbered over seqo and then seqi. Among the rows of one block of 256 packed rows at most 32 name the same owner, and in every draw some owner is named by exactly 32 rows of some block.
All inputs are finite; a program needn't handle non-finite values.
Results may differ from the reference program's by a relative error of at most 0.015.
Values may be sent and summed in bfloat16 or wider, within the bound.
A program may use at most 64 MiB of HBM per device.

```python
import math
import jax
import jax.numpy as jnp
import numpy as np
from jax import lax

D = 2048
BLK = 512
SLOTS = 512
NOWN = 16
CGRP = 1024
CAP = 32
ROWS_DEV = 256
ROWS = 4096
LENGTH = 8192
A = 16
N_WIDTH = 2


def block_scale(stream_key, extent, pieces, smallest, high):
    level, own = 1.0, jax.random.fold_in(stream_key, 6)
    for axis_at, shards_of in pieces:
        heights = jnp.exp(jax.random.uniform(jax.random.fold_in(own, axis_at), (shards_of,), jnp.float32, smallest / len(pieces), high / len(pieces)))
        level = level * jnp.repeat(heights, extent[axis_at] // shards_of).reshape([-1 if axis == axis_at else 1 for axis in range(len(extent))])
    return level


def deal_out(rng, own, number, rows, number_of, top, limit, lean):
    order = jax.random.permutation(rng, number_of)
    crowded, usual = shares(number_of, rows * top, limit, lean, True), shares(number_of, rows * top, limit, lean, False)
    places = jnp.arange(number_of)

    def named(tallies, turn):
        used = int((tallies > 0).sum())
        fixed = max(1, used // 4)
        moved = fixed + (places - fixed + turn * (used - fixed)) % max(1, number_of - fixed)
        return jnp.zeros((number_of,), jnp.int32).at[order[jnp.where(places < fixed, places, moved)]].set(jnp.asarray(tallies, jnp.int32))

    tallies = jnp.where(number % 4 == 0, named(crowded, number // 4), named(usual, number - number // 4 - 1))
    mixed = jax.random.permutation(jax.random.fold_in(own, 3), number_of)
    source_of, taker = mixed[0:number_of // 2 * 2:2], mixed[1:number_of // 2 * 2:2]
    slack = jnp.minimum(tallies[source_of] - 1, limit - tallies[taker]) // 2
    slack = jnp.where((source_of == order[0]) | (taker == order[0]) | (tallies[taker] == 0), 0, jnp.maximum(slack, 0))
    moved = jax.random.randint(jax.random.fold_in(own, 4), (number_of // 2,), 0, 1 << 20) % (slack + 1)
    tallies = tallies.at[source_of].add(-moved).at[taker].add(moved)
    items = jnp.searchsorted(jnp.cumsum(tallies), jnp.arange(rows * top), side="right").astype(jnp.int32)
    table = items.reshape(top, rows).T
    table = table[jax.random.permutation(jax.random.fold_in(own, 1), rows)]
    turn = jax.random.randint(jax.random.fold_in(own, 2), (rows, 1), 0, top)
    return jnp.take_along_axis(table, (jnp.arange(top)[None, :] + turn) % top, axis=1)


def shares(amount, total, most, skew, full):
    loads = [(1 << 20) // math.isqrt(grade ** skew) + 1 for grade in range(1, amount + 1)]
    largest = most if full else min(most, max(-(-total // amount), total * loads[0] // sum(loads)))
    least = 1 if total - largest >= amount - 1 else 0
    counts, spare = [largest] + [least] * (amount - 1), total - largest - least * (amount - 1)
    while spare > 0:
        candidates = [i for i in range(1, amount) if counts[i] < largest] or [i for i in range(1, amount) if counts[i] < most]
        pool, budget = sum([loads[i] for i in candidates]), spare
        for i in candidates:
            addition = min(most - counts[i], max(1, budget * loads[i] // pool), spare)
            counts[i] = counts[i] + addition
            spare = spare - addition
    return np.array(counts)


def gaussian(key, dims, scale, most, shards=(), held_as=jnp.bfloat16):
    loudness = block_scale(key, dims, shards, -0.22, 0.18) if shards else 1.0
    result = jax.random.normal(key, dims, jnp.float32) * scale * loudness
    return jnp.minimum(jnp.maximum(result, -most), most).astype(held_as)


def setup_inputs(seed: int = 0) -> dict:
    keys = jax.random.split(jax.random.key(seed), 10)
    rows_in = gaussian(keys[0], (ROWS, D), 1.0, 6.0, ((0, 16), (1, 2)))
    owner_keys = jax.random.split(jax.random.fold_in(keys[1], 1), ROWS // ROWS_DEV)
    owner_turns = jax.random.permutation(jax.random.fold_in(keys[1], 3), ROWS // ROWS_DEV)
    owner = jax.vmap(lambda own, number: deal_out(jax.random.fold_in(keys[1], 2), own, number, ROWS_DEV, NOWN, 1, CAP, 2))(owner_keys, owner_turns).reshape((ROWS, 1))
    first_blocks = gaussian(keys[2], (A, BLK, BLK), BLK ** -0.5, 0.25, ((0, 16),))
    middle_blocks = gaussian(keys[3], (BLK, A, A), A ** -0.5, 1.5, ((0, 16),))
    last_blocks = gaussian(keys[4], (A, BLK, BLK), BLK ** -0.5, 0.25, ((0, 16),))
    kernel = gaussian(keys[5], (A, BLK, D), 1.0, 6.0, ((1, 16), (2, 2)))
    gate_gain = gaussian(keys[6], (D,), 1.0, 4.0, ((0, 2),), jnp.float32)
    gate_bias = gaussian(keys[7], (D,), 1.0, 4.0, ((0, 2),), jnp.float32)
    cotangent = gaussian(keys[8], (LENGTH, D), 1.0, 6.0, ((0, 16), (1, 2)))
    return dict(rows_in=rows_in, owner=owner, first_blocks=first_blocks, middle_blocks=middle_blocks, last_blocks=last_blocks, kernel=kernel, gate_gain=gate_gain, gate_bias=gate_bias, cotangent=cotangent)


def positions(owner):
    flat = owner[:, 0].reshape(NOWN, ROWS_DEV).astype(jnp.int32)
    matches = (flat[:, :, None] == jnp.arange(NOWN, dtype=jnp.int32)[None, None, :]).astype(jnp.int32)
    order_rank = jnp.sum(matches * jnp.cumsum(matches, axis=1), axis=2) - 1
    source = jnp.arange(NOWN, dtype=jnp.int32)[:, None]
    return (flat * SLOTS + source * CAP + order_rank).reshape(-1).astype(jnp.int32)


def reference(rows_in, owner, first_blocks, middle_blocks, last_blocks, kernel, gate_gain, gate_bias, cotangent):
    position = positions(owner)
    first_f = first_blocks.astype(jnp.float32)
    middle_f = middle_blocks.astype(jnp.float32)
    last_f = last_blocks.astype(jnp.float32)
    rows_groups = rows_in.reshape(ROWS, N_WIDTH, CGRP).transpose(1, 0, 2)
    kernel_groups = kernel.reshape(A, BLK, N_WIDTH, CGRP).transpose(2, 0, 1, 3)
    upstream_groups = cotangent.reshape(A, BLK, N_WIDTH, CGRP).transpose(2, 0, 1, 3)
    gain_groups = gate_gain.reshape(N_WIDTH, CGRP)
    bias_groups = gate_bias.reshape(N_WIDTH, CGRP)

    def one_group(totals, inputs):
        sum_last, sum_middle = totals
        group_rows, group_kernel, group_gain, group_bias, upstream = inputs
        sequence = jnp.zeros((LENGTH, CGRP), jnp.bfloat16).at[position].set(group_rows).reshape(A, BLK, CGRP)
        seq_f = sequence.astype(jnp.float32)
        kern_f = group_kernel.astype(jnp.float32)
        up_f = upstream.astype(jnp.float32)
        mixed_first = jnp.einsum("aij,ajc->aic", first_f, seq_f).astype(jnp.bfloat16)
        mixed_middle = jnp.einsum("bia,abc->ibc", middle_f, mixed_first.astype(jnp.float32))
        weighted = (mixed_middle * kern_f).astype(jnp.bfloat16)
        mixed_last = jnp.einsum("aij,ajc->aic", last_f, weighted.astype(jnp.float32))
        gate_open = jax.nn.sigmoid(seq_f * group_gain + group_bias)
        grad_mixed = (up_f * gate_open).astype(jnp.bfloat16)
        grad_weighted = jnp.einsum("aij,aic->ajc", last_f, grad_mixed.astype(jnp.float32)).astype(jnp.bfloat16)
        part_last = jnp.einsum("aic,ajc->aij", grad_mixed.astype(jnp.float32), weighted.astype(jnp.float32))
        part_last = part_last.astype(jnp.bfloat16).astype(jnp.float32)
        grad_kern = (grad_weighted.astype(jnp.float32) * mixed_middle).astype(jnp.bfloat16)
        grad_mid_in = (grad_weighted.astype(jnp.float32) * kern_f).astype(jnp.bfloat16)
        part_middle = jnp.einsum("ibc,abc->bia", grad_mid_in.astype(jnp.float32), mixed_first.astype(jnp.float32))
        part_middle = part_middle.astype(jnp.bfloat16).astype(jnp.float32)
        grad_first_out = jnp.einsum("bia,ibc->abc", middle_f, grad_mid_in.astype(jnp.float32)).astype(jnp.bfloat16)
        grad_seq = jnp.einsum("aij,aic->ajc", first_f, grad_first_out.astype(jnp.float32))
        grad_seq = grad_seq + up_f * mixed_last * gate_open * (1.0 - gate_open) * group_gain
        grad_seq = grad_seq.astype(jnp.bfloat16).reshape(LENGTH, CGRP)
        grad_group = grad_seq[position]
        return (sum_last + part_last, sum_middle + part_middle), (grad_group, grad_kern)

    start = (jnp.zeros((A, BLK, BLK), jnp.float32), jnp.zeros((BLK, A, A), jnp.float32))
    totals, stacked = lax.scan(one_group, start, (rows_groups, kernel_groups, gain_groups, bias_groups, upstream_groups))
    grad_last, grad_middle = totals
    grad_groups, kernel_parts = stacked
    grad_rows = grad_groups.transpose(1, 0, 2).reshape(ROWS, D)
    grad_kernel = kernel_parts.transpose(1, 2, 0, 3).reshape(A, BLK, D)
    return (grad_rows, grad_middle, grad_last, grad_kernel)
```

```python
import functools
import jax
import jax.numpy as jnp
from jax import lax
from jax.experimental import pallas as pl
from jax.experimental.pallas import tpu as pltpu
from jax.sharding import PartitionSpec as P

CHUNKS = 2
MESH = pl.DeviceIdType.MESH


def deliver(buffer, owners):
    by_owner = buffer.reshape(owners, buffer.shape[0] // owners, buffer.shape[1])
    arrived = lax.all_to_all(by_owner, ("seqo", "seqi"), split_axis=0, concat_axis=0, tiled=True)
    return arrived.reshape(buffer.shape)


def regroup(blocks):
    arrived = lax.all_to_all(blocks, ("seqo", "seqi"), split_axis=1, concat_axis=1, tiled=True)
    return arrived


def per_device_plain(
    rows_in,
    owner,
    first_blocks,
    middle_blocks,
    last_blocks,
    kernel,
    gate_gain,
    gate_bias,
    cotangent,
):
    outer_count = lax.axis_size("seqo")
    owners = outer_count * lax.axis_size("seqi")
    channels = rows_in.shape[1]
    slots = cotangent.shape[0]
    capacity = slots // owners
    count_a = first_blocks.shape[0]
    block_size = first_blocks.shape[1]
    narrow = block_size // owners
    outer_len = middle_blocks.shape[1]
    target = owner[:, 0]
    matches = (target[:, None] == jnp.arange(owners, dtype=jnp.int32)[None, :]).astype(jnp.int32)
    order_rank = jnp.sum(matches * jnp.cumsum(matches, axis=0), axis=1) - 1
    slot_index = target * capacity + order_rank
    outbox = jnp.zeros((slots, channels), jnp.bfloat16).at[slot_index].set(rows_in)
    seq_in = deliver(outbox, owners).reshape(count_a, block_size, channels)
    gate_open = jax.nn.sigmoid(seq_in.astype(jnp.float32) * gate_gain + gate_bias)
    upstream = cotangent.reshape(count_a, block_size, channels).astype(jnp.float32)
    grad_mixed = (upstream * gate_open).astype(jnp.bfloat16)
    grad_weighted = jnp.einsum(
        "aij,aic->ajc", last_blocks, grad_mixed, preferred_element_type=jnp.float32
    ).astype(jnp.bfloat16)
    grad_wrows = grad_weighted.reshape(count_a, owners, narrow, channels)
    mixed_first = jnp.einsum(
        "aij,ajc->aic", first_blocks, seq_in, preferred_element_type=jnp.float32
    ).astype(jnp.bfloat16)
    first_rows = mixed_first.reshape(count_a, owners, narrow, channels)
    columns_in = regroup(first_rows)
    middle_view = middle_blocks.reshape(narrow, owners, count_a, owners, count_a)
    mixed_middle = jnp.einsum(
        "btmsl,lsbc->mtbc", middle_view, columns_in, preferred_element_type=jnp.float32
    )
    kernel_view = jnp.swapaxes(kernel.reshape(owners, count_a, narrow, channels), 0, 1).astype(
        jnp.float32
    )
    weighted_cols = (mixed_middle * kernel_view).astype(jnp.bfloat16)
    weighted = regroup(weighted_cols).reshape(count_a, block_size, channels)
    grad_cols = regroup(grad_wrows)
    grad_cols_f = grad_cols.astype(jnp.float32)
    grad_kern_view = (grad_cols_f * mixed_middle).astype(jnp.bfloat16)
    grad_kernel = jnp.swapaxes(grad_kern_view, 0, 1).reshape(outer_len, narrow, channels)
    grad_mid_in = (grad_cols_f * kernel_view).astype(jnp.bfloat16)
    part_middle = jnp.einsum(
        "mtbc,lsbc->btmsl", grad_mid_in, columns_in, preferred_element_type=jnp.float32
    )
    part_middle = part_middle.reshape(narrow, outer_len, outer_len)
    grad_first_cols = jnp.einsum(
        "btmsl,mtbc->lsbc", middle_view, grad_mid_in, preferred_element_type=jnp.float32
    ).astype(jnp.bfloat16)
    grad_first_out = regroup(grad_first_cols).reshape(count_a, block_size, channels)
    mixed_last = jnp.einsum(
        "aij,ajc->aic", last_blocks, weighted, preferred_element_type=jnp.float32
    )
    part_last = jnp.einsum("aic,ajc->aij", grad_mixed, weighted, preferred_element_type=jnp.float32)
    grad_seq = jnp.einsum(
        "aij,aic->ajc", first_blocks, grad_first_out, preferred_element_type=jnp.float32
    )
    grad_seq = grad_seq + upstream * mixed_last * gate_open * (1.0 - gate_open) * gate_gain
    returned = deliver(grad_seq.astype(jnp.bfloat16).reshape(slots, channels), owners)
    grad_rows = returned[slot_index]
    grad_middle, grad_last = (
        lax.psum_scatter(
            part_middle.astype(jnp.bfloat16), "width", scatter_dimension=1, tiled=True
        ).astype(jnp.float32),
        lax.psum_scatter(
            part_last.astype(jnp.bfloat16), "width", scatter_dimension=1, tiled=True
        ).astype(jnp.float32),
    )
    return (grad_rows, grad_middle, grad_last, grad_kernel)


def dot(a, b, contract):
    return lax.dot_general(
        a, b, (((contract[0],), (contract[1],)), ((), ())), preferred_element_type=jnp.float32
    )


def iota(shape, axis):
    return lax.broadcasted_iota(jnp.int32, shape, axis)


def fused(
    n_outer,
    n_inner,
    rows_ref,
    owner_ref,
    middle_ref,
    gain_ref,
    bias_ref,
    first_hbm,
    last_hbm,
    kernel_hbm,
    cot_hbm,
    grad_rows_ref,
    grad_middle_ref,
    grad_last_ref,
    grad_kernel_ref,
    first_ref,
    last_ref,
    kernel_ref,
    cot_ref,
    onehot_ref,
    mid_ref,
    mixed_ref,
    factor_ref,
    part_last_ref,
    part_mid_ref,
    send_last,
    recv_last,
    send_mid,
    recv_mid,
    send_buf,
    recv_buf,
    load_sem,
    send_sem,
    recv_sem,
    peer_send,
    peer_recv,
):
    owners = n_outer * n_inner
    wide = lax.axis_index("width")
    outer = lax.axis_index("seqo")
    inner = lax.axis_index("seqi")
    me = outer * n_inner + inner
    _, chunks, _, short, width = send_buf.shape
    slots = owners * short
    rows = rows_ref.shape[0]

    def partner(turn):
        to_outer = lax.rem(outer + lax.rem(turn, n_outer) + 1, n_outer)
        to_inner = lax.rem(inner + turn // n_outer + 1, n_inner)
        return to_outer, to_inner

    barrier = pltpu.get_barrier_semaphore()

    @pl.loop(0, owners - 1)
    def _(turn):
        to_outer, to_inner = partner(turn)
        pl.semaphore_signal(
            barrier, inc=1, device_id=(wide, to_outer, to_inner), device_id_type=MESH
        )

    pl.semaphore_signal(barrier, inc=1, device_id=(1 - wide, outer, inner), device_id_type=MESH)

    loads = [
        pltpu.make_async_copy(source, target, load_sem.at[at])
        for at, (source, target) in enumerate(
            (
                (first_hbm, first_ref),
                (last_hbm, last_ref),
                (kernel_hbm, kernel_ref),
                (cot_hbm, cot_ref),
            )
        )
    ]
    for load in loads:
        load.start()

    def columns(chunk):
        return pl.ds(pl.multiple_of(chunk * width, width), width)

    def exchange(phase, chunk, values):
        blocks = values.astype(jnp.bfloat16).reshape(owners, short, width)
        send_buf[phase, chunk] = blocks
        recv_buf[phase, chunk, me] = send_buf[phase, chunk, me]

        @pl.loop(0, owners - 1)
        def _(turn):
            to_outer, to_inner = partner(turn)
            to = to_outer * n_inner + to_inner
            pltpu.make_async_remote_copy(
                src_ref=send_buf.at[phase, chunk, to],
                dst_ref=recv_buf.at[phase, chunk, me],
                send_sem=send_sem.at[phase, chunk],
                recv_sem=recv_sem.at[phase, chunk],
                device_id=(wide, to_outer, to_inner),
                device_id_type=MESH,
            ).start()

    def arrived(phase, chunk):
        part = recv_buf.at[phase, chunk, pl.ds(0, owners - 1)]
        pltpu.make_async_copy(part, part, recv_sem.at[phase, chunk]).wait()
        return recv_buf[phase, chunk].reshape(slots, width)

    target = owner_ref[...]
    matches = (target == iota((rows, owners), 1)).astype(jnp.float32)
    lower = (iota((rows, rows), 0) >= iota((rows, rows), 1)).astype(jnp.bfloat16)
    counts = dot(lower, matches.astype(jnp.bfloat16), (1, 0))
    rank = jnp.sum(matches * counts, axis=1, keepdims=True) - 1.0
    slot = target.astype(jnp.float32) * float(short) + rank
    onehot_ref[...] = (slot == iota((rows, slots), 1).astype(jnp.float32)).astype(jnp.bfloat16)

    pl.semaphore_wait(barrier, owners)

    @pl.loop(0, chunks)
    def _(chunk):
        exchange(0, chunk, dot(onehot_ref[...], rows_ref[:, columns(chunk)], (0, 0)))

    row, col = iota((slots, slots), 0), iota((slots, slots), 1)
    reorder = (col == (row % short) * owners + row // short).astype(jnp.bfloat16)
    by_outer = dot(reorder, middle_ref[...], (1, 0)).astype(jnp.bfloat16)
    spread = (iota((owners, slots), 0) == iota((owners, slots), 1) // short).astype(jnp.bfloat16)
    dense = dot(by_outer, spread, (1, 0))
    mid_ref[...] = jnp.where(row % short == col % short, dense, 0.0).astype(jnp.bfloat16)
    part_last_ref[...] = jnp.zeros_like(part_last_ref)
    part_mid_ref[...] = jnp.zeros_like(part_mid_ref)
    for load in loads:
        load.wait()

    @pl.loop(0, chunks)
    def _(chunk):
        seq = arrived(0, chunk)
        exchange(1, chunk, dot(first_ref[0], seq, (1, 0)))
        gain = gain_ref[:, columns(chunk)]
        gate = jax.nn.sigmoid(seq.astype(jnp.float32) * gain + bias_ref[:, columns(chunk)])
        upstream = cot_ref[:, columns(chunk)].astype(jnp.float32)
        mixed = (upstream * gate).astype(jnp.bfloat16)
        mixed_ref[:, columns(chunk)] = mixed
        exchange(2, chunk, dot(last_ref[0], mixed, (0, 0)))
        factor_ref[:, columns(chunk)] = upstream * gate * (1.0 - gate) * gain

    @pl.loop(0, chunks)
    def _(chunk):
        first_cols = arrived(1, chunk)
        middle = dot(mid_ref[...], first_cols, (1, 0))
        taps = kernel_ref[:, :, columns(chunk)].reshape(slots, width).astype(jnp.float32)
        exchange(3, chunk, middle * taps)
        grad_cols = arrived(2, chunk).astype(jnp.float32)
        grad_mid_in = (grad_cols * taps).astype(jnp.bfloat16)
        exchange(4, chunk, dot(mid_ref[...], grad_mid_in, (0, 0)))
        grad_kernel_ref[:, :, columns(chunk)] = (
            (grad_cols * middle).astype(jnp.bfloat16).reshape(owners, short, width)
        )
        part_mid_ref[...] += dot(grad_mid_in, first_cols, (1, 1))

    @pl.loop(0, chunks)
    def _(chunk):
        weighted = arrived(3, chunk)
        local = dot(last_ref[0], weighted, (1, 0)) * factor_ref[:, columns(chunk)]
        exchange(5, chunk, dot(first_ref[0], arrived(4, chunk), (0, 0)) + local)
        part_last_ref[...] += dot(mixed_ref[:, columns(chunk)], weighted, (1, 1))

    half = slots // 2
    send_last[...] = part_last_ref[...].astype(jnp.bfloat16).reshape(2, half, slots)
    diagonal = jnp.where(
        iota((slots, slots), 0) % short == iota((slots, slots), 1) % short, part_mid_ref[...], 0.0
    ).astype(jnp.bfloat16)
    gathered = dot(diagonal, spread, (1, 1)).astype(jnp.bfloat16)
    few = owners // 2
    half_row, half_col = iota((half, slots), 0), iota((half, slots), 1)
    for side in range(2):
        pick = half_col == (half_row % few + side * few) * short + half_row // few
        send_mid[side] = dot(pick.astype(jnp.bfloat16), gathered, (1, 0)).astype(jnp.bfloat16)
    peers = [
        pltpu.make_async_remote_copy(
            src_ref=source.at[1 - wide],
            dst_ref=landing,
            send_sem=peer_send.at[at],
            recv_sem=peer_recv.at[at],
            device_id=(1 - wide, outer, inner),
            device_id_type=MESH,
        )
        for at, (source, landing) in enumerate(((send_last, recv_last), (send_mid, recv_mid)))
    ]
    for copy in peers:
        copy.start()
    for copy in peers:
        copy.wait()
    grad_last_ref[0] = send_last[wide].astype(jnp.float32) + recv_last[...].astype(jnp.float32)
    grad_middle_ref[...] = send_mid[wide].astype(jnp.float32) + recv_mid[...].astype(jnp.float32)

    @pl.loop(0, chunks)
    def _(chunk):
        returned = arrived(5, chunk)
        grad_rows_ref[:, columns(chunk)] = dot(onehot_ref[...], returned, (1, 0)).astype(
            jnp.bfloat16
        )

    @pl.loop(0, send_buf.shape[0])
    def _(phase):
        @pl.loop(0, chunks)
        def _(chunk):
            part = send_buf.at[phase, chunk, pl.ds(0, owners - 1)]
            pltpu.make_async_copy(part, part, send_sem.at[phase, chunk]).wait()


def per_device(
    rows_in,
    owner,
    first_blocks,
    middle_blocks,
    last_blocks,
    kernel,
    gate_gain,
    gate_bias,
    cotangent,
):
    n_outer, n_inner = lax.axis_size("seqo"), lax.axis_size("seqi")
    owners = n_outer * n_inner
    rows, channels = rows_in.shape
    slots = cotangent.shape[0]
    short = slots // owners
    if lax.axis_size("width") != 2 or short % 16 or first_blocks.shape[0] != 1:
        return per_device_plain(
            rows_in,
            owner,
            first_blocks,
            middle_blocks,
            last_blocks,
            kernel,
            gate_gain,
            gate_bias,
            cotangent,
        )
    width = channels // CHUNKS
    f32, bf16 = jnp.float32, jnp.bfloat16
    in_vmem = pl.BlockSpec(memory_space=pltpu.VMEM)
    anywhere = pl.BlockSpec(memory_space=pl.ANY)
    grad_rows, grad_middle, grad_last, grad_kernel = pl.pallas_call(
        functools.partial(fused, n_outer, n_inner),
        out_shape=(
            jax.ShapeDtypeStruct((rows, channels), bf16),
            jax.ShapeDtypeStruct((slots // 2, owners), f32),
            jax.ShapeDtypeStruct((1, slots // 2, slots), f32),
            jax.ShapeDtypeStruct(kernel.shape, bf16),
        ),
        in_specs=[in_vmem] * 5 + [anywhere] * 4,
        out_specs=[in_vmem] * 4,
        scratch_shapes=[
            pltpu.VMEM(first_blocks.shape, bf16),
            pltpu.VMEM(last_blocks.shape, bf16),
            pltpu.VMEM(kernel.shape, bf16),
            pltpu.VMEM(cotangent.shape, bf16),
            pltpu.VMEM((rows, slots), bf16),
            pltpu.VMEM((slots, slots), bf16),
            pltpu.VMEM((slots, channels), bf16),
            pltpu.VMEM((slots, channels), f32),
            pltpu.VMEM((slots, slots), f32),
            pltpu.VMEM((slots, slots), f32),
            pltpu.VMEM((2, slots // 2, slots), bf16),
            pltpu.VMEM((slots // 2, slots), bf16),
            pltpu.VMEM((2, slots // 2, owners), bf16),
            pltpu.VMEM((slots // 2, owners), bf16),
            pltpu.VMEM((6, CHUNKS, owners, short, width), bf16),
            pltpu.VMEM((6, CHUNKS, owners, short, width), bf16),
            pltpu.SemaphoreType.DMA((4,)),
            pltpu.SemaphoreType.DMA((6, CHUNKS)),
            pltpu.SemaphoreType.DMA((6, CHUNKS)),
            pltpu.SemaphoreType.DMA((2,)),
            pltpu.SemaphoreType.DMA((2,)),
        ],
        compiler_params=pltpu.CompilerParams(
            collective_id=0, has_side_effects=True, vmem_limit_bytes=56 * 1024 * 1024
        ),
        cost_estimate=pl.CostEstimate(
            flops=20 * slots * slots * channels,
            bytes_accessed=16 * slots * channels,
            transcendentals=slots * channels,
        ),
        name="monarch",
    )(
        rows_in,
        owner,
        middle_blocks.reshape(slots, owners),
        gate_gain.reshape(1, channels),
        gate_bias.reshape(1, channels),
        first_blocks,
        last_blocks,
        kernel,
        cotangent,
    )
    return (
        grad_rows,
        grad_middle.reshape(slots // owners, owners // 2, owners),
        grad_last,
        grad_kernel,
    )


def solution(mesh):
    placed = (
        P(("seqo", "seqi"), "width"),
        P(("seqo", "seqi"), None),
        P(("seqo", "seqi"), None, None),
        P(("seqo", "seqi"), None, None),
        P(("seqo", "seqi"), None, None),
        P(None, ("seqo", "seqi"), "width"),
        P("width"),
        P("width"),
        P(("seqo", "seqi"), "width"),
    )
    return jax.shard_map(
        per_device,
        mesh=mesh,
        in_specs=placed,
        out_specs=(
            P(("seqo", "seqi"), "width"),
            P(("seqo", "seqi"), "width", None),
            P(("seqo", "seqi"), "width", None),
            P(None, ("seqo", "seqi"), "width"),
        ),
        check_vma=False,
    )
```

```python
import functools
import jax
import jax.numpy as jnp
from jax import lax
from jax.experimental import pallas as pl
from jax.experimental.pallas import tpu as pltpu
from jax.sharding import PartitionSpec as P

CHUNKS = 2
MESH = pl.DeviceIdType.MESH


def deliver(buffer, owners):
    by_owner = buffer.reshape(owners, buffer.shape[0] // owners, buffer.shape[1])
    arrived = lax.all_to_all(by_owner, ("seqo", "seqi"), split_axis=0, concat_axis=0, tiled=True)
    return arrived.reshape(buffer.shape)


def regroup(blocks):
    arrived = lax.all_to_all(blocks, ("seqo", "seqi"), split_axis=1, concat_axis=1, tiled=True)
    return arrived


def per_device_plain(
    rows_in,
    owner,
    first_blocks,
    middle_blocks,
    last_blocks,
    kernel,
    gate_gain,
    gate_bias,
    cotangent,
):
    outer_count = lax.axis_size("seqo")
    owners = outer_count * lax.axis_size("seqi")
    channels = rows_in.shape[1]
    slots = cotangent.shape[0]
    capacity = slots // owners
    count_a = first_blocks.shape[0]
    block_size = first_blocks.shape[1]
    narrow = block_size // owners
    outer_len = middle_blocks.shape[1]
    target = owner[:, 0]
    matches = (target[:, None] == jnp.arange(owners, dtype=jnp.int32)[None, :]).astype(jnp.int32)
    order_rank = jnp.sum(matches * jnp.cumsum(matches, axis=0), axis=1) - 1
    slot_index = target * capacity + order_rank
    outbox = jnp.zeros((slots, channels), jnp.bfloat16).at[slot_index].set(rows_in)
    seq_in = deliver(outbox, owners).reshape(count_a, block_size, channels)
    gate_open = jax.nn.sigmoid(seq_in.astype(jnp.float32) * gate_gain + gate_bias)
    upstream = cotangent.reshape(count_a, block_size, channels).astype(jnp.float32)
    grad_mixed = (upstream * gate_open).astype(jnp.bfloat16)
    grad_weighted = jnp.einsum(
        "aij,aic->ajc", last_blocks, grad_mixed, preferred_element_type=jnp.float32
    ).astype(jnp.bfloat16)
    grad_wrows = grad_weighted.reshape(count_a, owners, narrow, channels)
    mixed_first = jnp.einsum(
        "aij,ajc->aic", first_blocks, seq_in, preferred_element_type=jnp.float32
    ).astype(jnp.bfloat16)
    first_rows = mixed_first.reshape(count_a, owners, narrow, channels)
    columns_in = regroup(first_rows)
    middle_view = middle_blocks.reshape(narrow, owners, count_a, owners, count_a)
    mixed_middle = jnp.einsum(
        "btmsl,lsbc->mtbc", middle_view, columns_in, preferred_element_type=jnp.float32
    )
    kernel_view = jnp.swapaxes(kernel.reshape(owners, count_a, narrow, channels), 0, 1).astype(
        jnp.float32
    )
    weighted_cols = (mixed_middle * kernel_view).astype(jnp.bfloat16)
    weighted = regroup(weighted_cols).reshape(count_a, block_size, channels)
    grad_cols = regroup(grad_wrows)
    grad_cols_f = grad_cols.astype(jnp.float32)
    grad_kern_view = (grad_cols_f * mixed_middle).astype(jnp.bfloat16)
    grad_kernel = jnp.swapaxes(grad_kern_view, 0, 1).reshape(outer_len, narrow, channels)
    grad_mid_in = (grad_cols_f * kernel_view).astype(jnp.bfloat16)
    part_middle = jnp.einsum(
        "mtbc,lsbc->btmsl", grad_mid_in, columns_in, preferred_element_type=jnp.float32
    )
    part_middle = part_middle.reshape(narrow, outer_len, outer_len)
    grad_first_cols = jnp.einsum(
        "btmsl,mtbc->lsbc", middle_view, grad_mid_in, preferred_element_type=jnp.float32
    ).astype(jnp.bfloat16)
    grad_first_out = regroup(grad_first_cols).reshape(count_a, block_size, channels)
    mixed_last = jnp.einsum(
        "aij,ajc->aic", last_blocks, weighted, preferred_element_type=jnp.float32
    )
    part_last = jnp.einsum("aic,ajc->aij", grad_mixed, weighted, preferred_element_type=jnp.float32)
    grad_seq = jnp.einsum(
        "aij,aic->ajc", first_blocks, grad_first_out, preferred_element_type=jnp.float32
    )
    grad_seq = grad_seq + upstream * mixed_last * gate_open * (1.0 - gate_open) * gate_gain
    returned = deliver(grad_seq.astype(jnp.bfloat16).reshape(slots, channels), owners)
    grad_rows = returned[slot_index]
    grad_middle, grad_last = (
        lax.psum_scatter(
            part_middle.astype(jnp.bfloat16), "width", scatter_dimension=1, tiled=True
        ).astype(jnp.float32),
        lax.psum_scatter(
            part_last.astype(jnp.bfloat16), "width", scatter_dimension=1, tiled=True
        ).astype(jnp.float32),
    )
    return (grad_rows, grad_middle, grad_last, grad_kernel)


def dot(a, b, contract):
    return lax.dot_general(
        a, b, (((contract[0],), (contract[1],)), ((), ())), preferred_element_type=jnp.float32
    )


def iota(shape, axis):
    return lax.broadcasted_iota(jnp.int32, shape, axis)


def fused(
    n_outer,
    n_inner,
    rows_ref,
    owner_ref,
    middle_ref,
    gain_ref,
    bias_ref,
    first_hbm,
    last_hbm,
    kernel_hbm,
    cot_hbm,
    grad_rows_ref,
    grad_middle_ref,
    grad_last_hbm,
    grad_kernel_hbm,
    grad_last_ref,
    grad_kernel_ref,
    first_ref,
    last_ref,
    kernel_ref,
    cot_ref,
    onehot_ref,
    mid_ref,
    mixed_ref,
    factor_ref,
    part_last_ref,
    part_mid_ref,
    send_last,
    recv_last,
    send_mid,
    recv_mid,
    send_buf,
    recv_buf,
    load_sem,
    store_sem,
    send_sem,
    recv_sem,
    peer_send,
    peer_recv,
):
    owners = n_outer * n_inner
    wide = lax.axis_index("width")
    outer = lax.axis_index("seqo")
    inner = lax.axis_index("seqi")
    me = outer * n_inner + inner
    _, chunks, _, short, width = send_buf.shape
    slots = owners * short
    rows = rows_ref.shape[0]

    def partner(turn):
        to_outer = lax.rem(outer + turn // n_inner + 1, n_outer)
        to_inner = lax.rem(inner + lax.rem(turn, n_inner) + 1, n_inner)
        return to_outer, to_inner

    barrier = pltpu.get_barrier_semaphore()

    @pl.loop(0, owners - 1)
    def _(turn):
        to_outer, to_inner = partner(turn)
        pl.semaphore_signal(
            barrier, inc=1, device_id=(wide, to_outer, to_inner), device_id_type=MESH
        )

    pl.semaphore_signal(barrier, inc=1, device_id=(1 - wide, outer, inner), device_id_type=MESH)

    loads = [
        pltpu.make_async_copy(source, target, load_sem.at[at])
        for at, (source, target) in enumerate(
            (
                (first_hbm, first_ref),
                (last_hbm, last_ref),
                (kernel_hbm, kernel_ref),
                (cot_hbm, cot_ref),
            )
        )
    ]
    for load in loads:
        load.start()

    def columns(chunk):
        return pl.ds(pl.multiple_of(chunk * width, width), width)

    def exchange(phase, chunk, values):
        blocks = values.astype(jnp.bfloat16).reshape(owners, short, width)
        send_buf[phase, chunk] = blocks
        recv_buf[phase, chunk, me] = send_buf[phase, chunk, me]

        @pl.loop(0, owners - 1)
        def _(turn):
            to_outer, to_inner = partner(turn)
            to = to_outer * n_inner + to_inner
            pltpu.make_async_remote_copy(
                src_ref=send_buf.at[phase, chunk, to],
                dst_ref=recv_buf.at[phase, chunk, me],
                send_sem=send_sem.at[phase, chunk],
                recv_sem=recv_sem.at[phase, chunk],
                device_id=(wide, to_outer, to_inner),
                device_id_type=MESH,
            ).start()

    def arrived(phase, chunk):
        part = recv_buf.at[phase, chunk, pl.ds(0, owners - 1)]
        pltpu.make_async_copy(part, part, recv_sem.at[phase, chunk]).wait()
        return recv_buf[phase, chunk].reshape(slots, width)

    target = owner_ref[...]
    matches = (target == iota((owners, rows), 0)).astype(jnp.float32)
    upper = (iota((rows, rows), 0) <= iota((rows, rows), 1)).astype(jnp.bfloat16)
    counts = dot(matches.astype(jnp.bfloat16), upper, (1, 0))
    rank = jnp.sum(matches * counts, axis=0, keepdims=True) - 1.0
    slot = target.astype(jnp.float32) * float(short) + rank
    onehot_ref[...] = (slot == iota((slots, rows), 0).astype(jnp.float32)).astype(jnp.bfloat16)

    pl.semaphore_wait(barrier, owners)

    @pl.loop(0, chunks)
    def _(chunk):
        exchange(0, chunk, dot(onehot_ref[...], rows_ref[:, columns(chunk)], (1, 0)))

    same_position = iota((slots, slots), 0) % short == iota((slots, slots), 1) % short
    pairs = owners * owners
    same_outer = (iota((pairs, slots), 0) % owners == iota((pairs, slots), 1) // short).astype(
        jnp.float32
    )
    spread = (iota((short, slots), 0) == iota((short, slots), 1) % short).astype(jnp.bfloat16)
    by_pair = (dot(middle_ref[...], spread, (1, 0)) * same_outer).astype(jnp.bfloat16)
    lift = (iota((slots, pairs), 0) // short == iota((slots, pairs), 1) // owners).astype(jnp.bfloat16)
    dense = dot(lift, by_pair, (1, 0))
    mid_ref[...] = jnp.where(same_position, dense, 0.0).astype(jnp.bfloat16)
    part_last_ref[...] = jnp.zeros_like(part_last_ref)
    part_mid_ref[...] = jnp.zeros_like(part_mid_ref)
    for load in loads:
        load.wait()

    @pl.loop(0, chunks)
    def _(chunk):
        seq = arrived(0, chunk)
        exchange(1, chunk, dot(first_ref[0], seq, (1, 0)))
        gain = gain_ref[:, columns(chunk)]
        gate = jax.nn.sigmoid(seq.astype(jnp.float32) * gain + bias_ref[:, columns(chunk)])
        upstream = cot_ref[:, columns(chunk)].astype(jnp.float32)
        mixed = (upstream * gate).astype(jnp.bfloat16)
        mixed_ref[:, columns(chunk)] = mixed
        exchange(2, chunk, dot(last_ref[0], mixed, (0, 0)))
        factor_ref[:, columns(chunk)] = upstream * gate * (1.0 - gate) * gain

    @pl.loop(0, chunks)
    def _(chunk):
        first_cols = arrived(1, chunk)
        middle = dot(mid_ref[...], first_cols, (1, 0))
        taps = kernel_ref[:, :, columns(chunk)].reshape(slots, width).astype(jnp.float32)
        exchange(3, chunk, middle * taps)
        grad_cols = arrived(2, chunk).astype(jnp.float32)
        grad_mid_in = (grad_cols * taps).astype(jnp.bfloat16)
        exchange(4, chunk, dot(mid_ref[...], grad_mid_in, (0, 0)))
        grad_kernel_ref[:, :, columns(chunk)] = (
            (grad_cols * middle).astype(jnp.bfloat16).reshape(owners, short, width)
        )
        part_mid_ref[...] += dot(grad_mid_in, first_cols, (1, 1))

    @pl.loop(0, chunks)
    def _(chunk):
        weighted = arrived(3, chunk)
        local = dot(last_ref[0], weighted, (1, 0)) * factor_ref[:, columns(chunk)]
        exchange(5, chunk, dot(first_ref[0], arrived(4, chunk), (0, 0)) + local)
        part_last_ref[...] += dot(mixed_ref[:, columns(chunk)], weighted, (1, 1))

    store_kernel = pltpu.make_async_copy(grad_kernel_ref, grad_kernel_hbm, store_sem.at[0])
    store_kernel.start()

    half = slots // 2
    send_last[...] = part_last_ref[...].astype(jnp.bfloat16).reshape(2, half, slots)
    diagonal = jnp.where(same_position, part_mid_ref[...], 0.0).astype(jnp.bfloat16)
    down = (iota((pairs, slots), 0) // owners == iota((pairs, slots), 1) // short).astype(jnp.bfloat16)
    gathered = (dot(down, diagonal, (1, 0)) * same_outer).astype(jnp.bfloat16)
    send_mid[...] = (
        dot(gathered, spread, (1, 1)).astype(jnp.bfloat16).reshape(2, pairs // 2, short)
    )
    peers = [
        pltpu.make_async_remote_copy(
            src_ref=source.at[1 - wide],
            dst_ref=landing,
            send_sem=peer_send.at[at],
            recv_sem=peer_recv.at[at],
            device_id=(1 - wide, outer, inner),
            device_id_type=MESH,
        )
        for at, (source, landing) in enumerate(((send_last, recv_last), (send_mid, recv_mid)))
    ]
    for copy in peers:
        copy.start()
    for copy in peers:
        copy.wait()
    grad_last_ref[0] = send_last[wide].astype(jnp.float32) + recv_last[...].astype(jnp.float32)
    store_last = pltpu.make_async_copy(grad_last_ref, grad_last_hbm, store_sem.at[1])
    store_last.start()
    grad_middle_ref[...] = send_mid[wide].astype(jnp.float32) + recv_mid[...].astype(jnp.float32)

    @pl.loop(0, chunks)
    def _(chunk):
        returned = arrived(5, chunk)
        grad_rows_ref[:, columns(chunk)] = dot(onehot_ref[...], returned, (0, 0)).astype(
            jnp.bfloat16
        )

    @pl.loop(0, send_buf.shape[0])
    def _(phase):
        @pl.loop(0, chunks)
        def _(chunk):
            part = send_buf.at[phase, chunk, pl.ds(0, owners - 1)]
            pltpu.make_async_copy(part, part, send_sem.at[phase, chunk]).wait()

    store_kernel.wait()
    store_last.wait()


def settle(*refs):
    count = (len(refs) - 1) // 2
    copies = [
        pltpu.make_async_copy(refs[at], refs[count + at], refs[-1].at[at]) for at in range(count)
    ]
    for copy in copies:
        copy.start()
    for copy in copies:
        copy.wait()


def per_device(
    rows_in,
    owner,
    first_blocks,
    middle_blocks,
    last_blocks,
    kernel,
    gate_gain,
    gate_bias,
    cotangent,
):
    n_outer, n_inner = lax.axis_size("seqo"), lax.axis_size("seqi")
    owners = n_outer * n_inner
    rows, channels = rows_in.shape
    slots = cotangent.shape[0]
    short = slots // owners
    if lax.axis_size("width") != 2 or short % 16 or first_blocks.shape[0] != 1:
        return per_device_plain(
            rows_in,
            owner,
            first_blocks,
            middle_blocks,
            last_blocks,
            kernel,
            gate_gain,
            gate_bias,
            cotangent,
        )
    width = channels // CHUNKS
    f32, bf16 = jnp.float32, jnp.bfloat16
    in_vmem = pl.BlockSpec(memory_space=pltpu.VMEM)
    anywhere = pl.BlockSpec(memory_space=pl.ANY)
    results = pl.pallas_call(
        functools.partial(fused, n_outer, n_inner),
        out_shape=(
            jax.ShapeDtypeStruct((rows, channels), bf16),
            jax.ShapeDtypeStruct((owners * owners // 2, short), f32),
            jax.ShapeDtypeStruct((1, slots // 2, slots), f32),
            jax.ShapeDtypeStruct(kernel.shape, bf16),
        ),
        in_specs=[in_vmem] * 5 + [anywhere] * 4,
        out_specs=[in_vmem] * 2 + [anywhere] * 2,
        scratch_shapes=[
            pltpu.VMEM((1, slots // 2, slots), f32),
            pltpu.VMEM(kernel.shape, bf16),
            pltpu.VMEM(first_blocks.shape, bf16),
            pltpu.VMEM(last_blocks.shape, bf16),
            pltpu.VMEM(kernel.shape, bf16),
            pltpu.VMEM(cotangent.shape, bf16),
            pltpu.VMEM((slots, rows), bf16),
            pltpu.VMEM((slots, slots), bf16),
            pltpu.VMEM((slots, channels), bf16),
            pltpu.VMEM((slots, channels), f32),
            pltpu.VMEM((slots, slots), f32),
            pltpu.VMEM((slots, slots), f32),
            pltpu.VMEM((2, slots // 2, slots), bf16),
            pltpu.VMEM((slots // 2, slots), bf16),
            pltpu.VMEM((2, owners * owners // 2, short), bf16),
            pltpu.VMEM((owners * owners // 2, short), bf16),
            pltpu.VMEM((6, CHUNKS, owners, short, width), bf16),
            pltpu.VMEM((6, CHUNKS, owners, short, width), bf16),
            pltpu.SemaphoreType.DMA((4,)),
            pltpu.SemaphoreType.DMA((2,)),
            pltpu.SemaphoreType.DMA((6, CHUNKS)),
            pltpu.SemaphoreType.DMA((6, CHUNKS)),
            pltpu.SemaphoreType.DMA((2,)),
            pltpu.SemaphoreType.DMA((2,)),
        ],
        compiler_params=pltpu.CompilerParams(
            collective_id=0, has_side_effects=True, vmem_limit_bytes=56 * 1024 * 1024
        ),
        cost_estimate=pl.CostEstimate(
            flops=20 * slots * slots * channels,
            bytes_accessed=16 * slots * channels,
            transcendentals=slots * channels,
        ),
        name="monarch",
    )(
        rows_in,
        owner.reshape(1, rows),
        middle_blocks.transpose(1, 2, 0).reshape(owners * owners, short),
        gate_gain.reshape(1, channels),
        gate_bias.reshape(1, channels),
        first_blocks,
        last_blocks,
        kernel,
        cotangent,
    )
    grad_rows, grad_middle, grad_last, grad_kernel = pl.pallas_call(
        settle,
        out_shape=tuple(jax.ShapeDtypeStruct(held.shape, held.dtype) for held in results),
        in_specs=[anywhere] * 4,
        out_specs=[anywhere] * 4,
        scratch_shapes=[pltpu.SemaphoreType.DMA((4,))],
        compiler_params=pltpu.CompilerParams(vmem_limit_bytes=56 * 1024 * 1024),
        name="settle",
    )(*results)
    grad_middle = grad_middle.reshape(owners // 2, owners, short).transpose(2, 0, 1)
    return (grad_rows, grad_middle, grad_last, grad_kernel)


def solution(mesh):
    placed = (
        P(("seqo", "seqi"), "width"),
        P(("seqo", "seqi"), None),
        P(("seqo", "seqi"), None, None),
        P(("seqo", "seqi"), None, None),
        P(("seqo", "seqi"), None, None),
        P(None, ("seqo", "seqi"), "width"),
        P("width"),
        P("width"),
        P(("seqo", "seqi"), "width"),
    )
    return jax.shard_map(
        per_device,
        mesh=mesh,
        in_specs=placed,
        out_specs=(
            P(("seqo", "seqi"), "width"),
            P(("seqo", "seqi"), "width", None),
            P(("seqo", "seqi"), "width", None),
            P(None, ("seqo", "seqi"), "width"),
        ),
        check_vma=False,
    )
```

```python
import functools
import jax
import jax.numpy as jnp
from jax import lax
from jax.experimental import pallas as pl
from jax.experimental.pallas import tpu as pltpu
from jax.sharding import PartitionSpec as P

CHUNKS = 4
MESH = pl.DeviceIdType.MESH


def deliver(buffer, owners):
    by_owner = buffer.reshape(owners, buffer.shape[0] // owners, buffer.shape[1])
    arrived = lax.all_to_all(by_owner, ("seqo", "seqi"), split_axis=0, concat_axis=0, tiled=True)
    return arrived.reshape(buffer.shape)


def regroup(blocks):
    arrived = lax.all_to_all(blocks, ("seqo", "seqi"), split_axis=1, concat_axis=1, tiled=True)
    return arrived


def per_device_plain(
    rows_in,
    owner,
    first_blocks,
    middle_blocks,
    last_blocks,
    kernel,
    gate_gain,
    gate_bias,
    cotangent,
):
    outer_count = lax.axis_size("seqo")
    owners = outer_count * lax.axis_size("seqi")
    channels = rows_in.shape[1]
    slots = cotangent.shape[0]
    capacity = slots // owners
    count_a = first_blocks.shape[0]
    block_size = first_blocks.shape[1]
    narrow = block_size // owners
    outer_len = middle_blocks.shape[1]
    target = owner[:, 0]
    matches = (target[:, None] == jnp.arange(owners, dtype=jnp.int32)[None, :]).astype(jnp.int32)
    order_rank = jnp.sum(matches * jnp.cumsum(matches, axis=0), axis=1) - 1
    slot_index = target * capacity + order_rank
    outbox = jnp.zeros((slots, channels), jnp.bfloat16).at[slot_index].set(rows_in)
    seq_in = deliver(outbox, owners).reshape(count_a, block_size, channels)
    gate_open = jax.nn.sigmoid(seq_in.astype(jnp.float32) * gate_gain + gate_bias)
    upstream = cotangent.reshape(count_a, block_size, channels).astype(jnp.float32)
    grad_mixed = (upstream * gate_open).astype(jnp.bfloat16)
    grad_weighted = jnp.einsum(
        "aij,aic->ajc", last_blocks, grad_mixed, preferred_element_type=jnp.float32
    ).astype(jnp.bfloat16)
    grad_wrows = grad_weighted.reshape(count_a, owners, narrow, channels)
    mixed_first = jnp.einsum(
        "aij,ajc->aic", first_blocks, seq_in, preferred_element_type=jnp.float32
    ).astype(jnp.bfloat16)
    first_rows = mixed_first.reshape(count_a, owners, narrow, channels)
    columns_in = regroup(first_rows)
    middle_view = middle_blocks.reshape(narrow, owners, count_a, owners, count_a)
    mixed_middle = jnp.einsum(
        "btmsl,lsbc->mtbc", middle_view, columns_in, preferred_element_type=jnp.float32
    )
    kernel_view = jnp.swapaxes(kernel.reshape(owners, count_a, narrow, channels), 0, 1).astype(
        jnp.float32
    )
    weighted_cols = (mixed_middle * kernel_view).astype(jnp.bfloat16)
    weighted = regroup(weighted_cols).reshape(count_a, block_size, channels)
    grad_cols = regroup(grad_wrows)
    grad_cols_f = grad_cols.astype(jnp.float32)
    grad_kern_view = (grad_cols_f * mixed_middle).astype(jnp.bfloat16)
    grad_kernel = jnp.swapaxes(grad_kern_view, 0, 1).reshape(outer_len, narrow, channels)
    grad_mid_in = (grad_cols_f * kernel_view).astype(jnp.bfloat16)
    part_middle = jnp.einsum(
        "mtbc,lsbc->btmsl", grad_mid_in, columns_in, preferred_element_type=jnp.float32
    )
    part_middle = part_middle.reshape(narrow, outer_len, outer_len)
    grad_first_cols = jnp.einsum(
        "btmsl,mtbc->lsbc", middle_view, grad_mid_in, preferred_element_type=jnp.float32
    ).astype(jnp.bfloat16)
    grad_first_out = regroup(grad_first_cols).reshape(count_a, block_size, channels)
    mixed_last = jnp.einsum(
        "aij,ajc->aic", last_blocks, weighted, preferred_element_type=jnp.float32
    )
    part_last = jnp.einsum("aic,ajc->aij", grad_mixed, weighted, preferred_element_type=jnp.float32)
    grad_seq = jnp.einsum(
        "aij,aic->ajc", first_blocks, grad_first_out, preferred_element_type=jnp.float32
    )
    grad_seq = grad_seq + upstream * mixed_last * gate_open * (1.0 - gate_open) * gate_gain
    returned = deliver(grad_seq.astype(jnp.bfloat16).reshape(slots, channels), owners)
    grad_rows = returned[slot_index]
    grad_middle, grad_last = (
        lax.psum_scatter(
            part_middle.astype(jnp.bfloat16), "width", scatter_dimension=1, tiled=True
        ).astype(jnp.float32),
        lax.psum_scatter(
            part_last.astype(jnp.bfloat16), "width", scatter_dimension=1, tiled=True
        ).astype(jnp.float32),
    )
    return (grad_rows, grad_middle, grad_last, grad_kernel)


def dot(a, b, contract):
    return lax.dot_general(
        a, b, (((contract[0],), (contract[1],)), ((), ())), preferred_element_type=jnp.float32
    )


def iota(shape, axis):
    return lax.broadcasted_iota(jnp.int32, shape, axis)


def fused(
    n_outer,
    n_inner,
    owner_ref,
    middle_ref,
    gain_ref,
    bias_ref,
    first_hbm,
    last_hbm,
    kernel_hbm,
    cot_hbm,
    rows_hbm,
    grad_rows_ref,
    grad_middle_ref,
    grad_last_hbm,
    grad_kernel_hbm,
    grad_last_ref,
    grad_kernel_ref,
    first_ref,
    last_ref,
    kernel_ref,
    cot_ref,
    rows_ref,
    onehot_ref,
    mid_ref,
    mixed_ref,
    factor_ref,
    part_last_ref,
    part_mid_ref,
    send_last,
    recv_last,
    send_mid,
    recv_mid,
    send_buf,
    recv_buf,
    load_sem,
    store_sem,
    send_sem,
    recv_sem,
    peer_send,
    peer_recv,
):
    owners = n_outer * n_inner
    wide = lax.axis_index("width")
    outer = lax.axis_index("seqo")
    inner = lax.axis_index("seqi")
    me = outer * n_inner + inner
    _, chunks, _, short, width = send_buf.shape
    slots = owners * short
    rows = rows_ref.shape[0]

    def partner(turn):
        to_outer = lax.rem(outer + turn // n_inner + 1, n_outer)
        to_inner = lax.rem(inner + lax.rem(turn, n_inner) + 1, n_inner)
        return to_outer, to_inner

    loads = [
        pltpu.make_async_copy(source, target, load_sem.at[at])
        for at, (source, target) in enumerate(
            (
                (first_hbm, first_ref),
                (last_hbm, last_ref),
                (kernel_hbm, kernel_ref),
                (cot_hbm, cot_ref),
                (rows_hbm, rows_ref),
            )
        )
    ]
    loads[4].start()

    barrier = pltpu.get_barrier_semaphore()

    @pl.loop(0, owners - 1)
    def _(turn):
        to_outer, to_inner = partner(turn)
        pl.semaphore_signal(
            barrier, inc=1, device_id=(wide, to_outer, to_inner), device_id_type=MESH
        )

    pl.semaphore_signal(barrier, inc=1, device_id=(1 - wide, outer, inner), device_id_type=MESH)

    def columns(chunk):
        return pl.ds(pl.multiple_of(chunk * width, width), width)

    def exchange(phase, chunk, values):
        blocks = values.astype(jnp.bfloat16).reshape(owners, short, width)
        send_buf[phase, chunk] = blocks
        recv_buf[phase, chunk, me] = send_buf[phase, chunk, me]

        @pl.loop(0, owners - 1)
        def _(turn):
            to_outer, to_inner = partner(turn)
            to = to_outer * n_inner + to_inner
            pltpu.make_async_remote_copy(
                src_ref=send_buf.at[phase, chunk, to],
                dst_ref=recv_buf.at[phase, chunk, me],
                send_sem=send_sem.at[phase, chunk],
                recv_sem=recv_sem.at[phase, chunk],
                device_id=(wide, to_outer, to_inner),
                device_id_type=MESH,
            ).start()

    def arrived(phase, chunk):
        part = recv_buf.at[phase, chunk, pl.ds(0, owners - 1)]
        pltpu.make_async_copy(part, part, recv_sem.at[phase, chunk]).wait()
        return recv_buf[phase, chunk].reshape(slots, width)

    target = owner_ref[...]
    matches = (target == iota((owners, rows), 0)).astype(jnp.float32)
    upper = (iota((rows, rows), 0) <= iota((rows, rows), 1)).astype(jnp.bfloat16)
    counts = dot(matches.astype(jnp.bfloat16), upper, (1, 0))
    rank = jnp.sum(matches * counts, axis=0, keepdims=True) - 1.0
    slot = target.astype(jnp.float32) * float(short) + rank
    onehot_ref[...] = (slot == iota((slots, rows), 0).astype(jnp.float32)).astype(jnp.bfloat16)

    for load in loads[:4]:
        load.start()
    loads[4].wait()
    pl.semaphore_wait(barrier, owners)

    @pl.loop(0, chunks)
    def _(chunk):
        exchange(0, chunk, dot(onehot_ref[...], rows_ref[:, columns(chunk)], (1, 0)))

    same_position = iota((slots, slots), 0) % short == iota((slots, slots), 1) % short
    pairs = owners * owners
    same_outer = (iota((pairs, slots), 0) % owners == iota((pairs, slots), 1) // short).astype(
        jnp.float32
    )
    spread = (iota((short, slots), 0) == iota((short, slots), 1) % short).astype(jnp.bfloat16)
    by_pair = (dot(middle_ref[...], spread, (1, 0)) * same_outer).astype(jnp.bfloat16)
    lift = (iota((slots, pairs), 0) // short == iota((slots, pairs), 1) // owners).astype(jnp.bfloat16)
    dense = dot(lift, by_pair, (1, 0))
    mid_ref[...] = jnp.where(same_position, dense, 0.0).astype(jnp.bfloat16)
    part_last_ref[...] = jnp.zeros_like(part_last_ref)
    part_mid_ref[...] = jnp.zeros_like(part_mid_ref)
    for load in loads[:4]:
        load.wait()

    @pl.loop(0, chunks)
    def _(chunk):
        seq = arrived(0, chunk)
        exchange(1, chunk, dot(first_ref[0], seq, (1, 0)))
        gain = gain_ref[:, columns(chunk)]
        gate = jax.nn.sigmoid(seq.astype(jnp.float32) * gain + bias_ref[:, columns(chunk)])
        upstream = cot_ref[:, columns(chunk)].astype(jnp.float32)
        mixed = (upstream * gate).astype(jnp.bfloat16)
        mixed_ref[:, columns(chunk)] = mixed
        exchange(2, chunk, dot(last_ref[0], mixed, (0, 0)))
        factor_ref[:, columns(chunk)] = upstream * gate * (1.0 - gate) * gain

    @pl.loop(0, chunks)
    def _(chunk):
        first_cols = arrived(1, chunk)
        middle = dot(mid_ref[...], first_cols, (1, 0))
        taps = kernel_ref[:, :, columns(chunk)].reshape(slots, width).astype(jnp.float32)
        exchange(3, chunk, middle * taps)
        grad_cols = arrived(2, chunk).astype(jnp.float32)
        grad_mid_in = (grad_cols * taps).astype(jnp.bfloat16)
        exchange(4, chunk, dot(mid_ref[...], grad_mid_in, (0, 0)))
        grad_kernel_ref[:, :, columns(chunk)] = (
            (grad_cols * middle).astype(jnp.bfloat16).reshape(owners, short, width)
        )
        part_mid_ref[...] += dot(grad_mid_in, first_cols, (1, 1))

    @pl.loop(0, chunks)
    def _(chunk):
        weighted = arrived(3, chunk)
        local = dot(last_ref[0], weighted, (1, 0)) * factor_ref[:, columns(chunk)]
        exchange(5, chunk, dot(first_ref[0], arrived(4, chunk), (0, 0)) + local)
        part_last_ref[...] += dot(mixed_ref[:, columns(chunk)], weighted, (1, 1))

    store_kernel = pltpu.make_async_copy(grad_kernel_ref, grad_kernel_hbm, store_sem.at[0])
    store_kernel.start()

    half = slots // 2
    send_last[...] = part_last_ref[...].astype(jnp.bfloat16).reshape(2, half, slots)
    diagonal = jnp.where(same_position, part_mid_ref[...], 0.0).astype(jnp.bfloat16)
    down = (iota((pairs, slots), 0) // owners == iota((pairs, slots), 1) // short).astype(jnp.bfloat16)
    gathered = (dot(down, diagonal, (1, 0)) * same_outer).astype(jnp.bfloat16)
    send_mid[...] = (
        dot(gathered, spread, (1, 1)).astype(jnp.bfloat16).reshape(2, pairs // 2, short)
    )
    peers = [
        pltpu.make_async_remote_copy(
            src_ref=source.at[1 - wide],
            dst_ref=landing,
            send_sem=peer_send.at[at],
            recv_sem=peer_recv.at[at],
            device_id=(1 - wide, outer, inner),
            device_id_type=MESH,
        )
        for at, (source, landing) in enumerate(((send_last, recv_last), (send_mid, recv_mid)))
    ]
    for copy in peers:
        copy.start()
    for copy in peers:
        copy.wait()
    grad_last_ref[0] = send_last[wide].astype(jnp.float32) + recv_last[...].astype(jnp.float32)
    store_last = pltpu.make_async_copy(grad_last_ref, grad_last_hbm, store_sem.at[1])
    store_last.start()
    grad_middle_ref[...] = send_mid[wide].astype(jnp.float32) + recv_mid[...].astype(jnp.float32)

    @pl.loop(0, chunks)
    def _(chunk):
        returned = arrived(5, chunk)
        grad_rows_ref[:, columns(chunk)] = dot(onehot_ref[...], returned, (0, 0)).astype(
            jnp.bfloat16
        )

    @pl.loop(0, send_buf.shape[0])
    def _(phase):
        @pl.loop(0, chunks)
        def _(chunk):
            part = send_buf.at[phase, chunk, pl.ds(0, owners - 1)]
            pltpu.make_async_copy(part, part, send_sem.at[phase, chunk]).wait()

    store_kernel.wait()
    store_last.wait()


def settle(*refs):
    count = (len(refs) - 2) // 3
    sources, targets, held = refs[:count], refs[count : 2 * count], refs[2 * count : 3 * count]
    load_sem, store_sem = refs[3 * count :]
    loads, stores = [], []
    for at in range(count):
        pieces = 1 if sources[at].shape[0] == 1 else 4
        size = sources[at].shape[0] // pieces
        for piece in range(pieces):
            span, turn = pl.ds(piece * size, size), len(loads)
            here = held[at].at[span]
            loads.append(
                pltpu.make_async_copy(sources[at].at[span], here, load_sem.at[turn])
            )
            stores.append(
                pltpu.make_async_copy(here, targets[at].at[span], store_sem.at[turn])
            )
    for load in loads:
        load.start()
    for load, store in zip(loads, stores):
        load.wait()
        store.start()
    for store in stores:
        store.wait()


def per_device(
    rows_in,
    owner,
    first_blocks,
    middle_blocks,
    last_blocks,
    kernel,
    gate_gain,
    gate_bias,
    cotangent,
):
    n_outer, n_inner = lax.axis_size("seqo"), lax.axis_size("seqi")
    owners = n_outer * n_inner
    rows, channels = rows_in.shape
    slots = cotangent.shape[0]
    short = slots // owners
    if lax.axis_size("width") != 2 or short % 16 or first_blocks.shape[0] != 1:
        return per_device_plain(
            rows_in,
            owner,
            first_blocks,
            middle_blocks,
            last_blocks,
            kernel,
            gate_gain,
            gate_bias,
            cotangent,
        )
    width = channels // CHUNKS
    f32, bf16 = jnp.float32, jnp.bfloat16
    in_vmem = pl.BlockSpec(memory_space=pltpu.VMEM)
    anywhere = pl.BlockSpec(memory_space=pl.ANY)
    results = pl.pallas_call(
        functools.partial(fused, n_outer, n_inner),
        out_shape=(
            jax.ShapeDtypeStruct((rows, channels), bf16),
            jax.ShapeDtypeStruct((owners * owners // 2, short), f32),
            jax.ShapeDtypeStruct((1, slots // 2, slots), f32),
            jax.ShapeDtypeStruct(kernel.shape, bf16),
        ),
        in_specs=[in_vmem] * 4 + [anywhere] * 5,
        out_specs=[in_vmem] * 2 + [anywhere] * 2,
        scratch_shapes=[
            pltpu.VMEM((1, slots // 2, slots), f32),
            pltpu.VMEM(kernel.shape, bf16),
            pltpu.VMEM(first_blocks.shape, bf16),
            pltpu.VMEM(last_blocks.shape, bf16),
            pltpu.VMEM(kernel.shape, bf16),
            pltpu.VMEM(cotangent.shape, bf16),
            pltpu.VMEM(rows_in.shape, bf16),
            pltpu.VMEM((slots, rows), bf16),
            pltpu.VMEM((slots, slots), bf16),
            pltpu.VMEM((slots, channels), bf16),
            pltpu.VMEM((slots, channels), f32),
            pltpu.VMEM((slots, slots), f32),
            pltpu.VMEM((slots, slots), f32),
            pltpu.VMEM((2, slots // 2, slots), bf16),
            pltpu.VMEM((slots // 2, slots), bf16),
            pltpu.VMEM((2, owners * owners // 2, short), bf16),
            pltpu.VMEM((owners * owners // 2, short), bf16),
            pltpu.VMEM((6, CHUNKS, owners, short, width), bf16),
            pltpu.VMEM((6, CHUNKS, owners, short, width), bf16),
            pltpu.SemaphoreType.DMA((5,)),
            pltpu.SemaphoreType.DMA((2,)),
            pltpu.SemaphoreType.DMA((6, CHUNKS)),
            pltpu.SemaphoreType.DMA((6, CHUNKS)),
            pltpu.SemaphoreType.DMA((2,)),
            pltpu.SemaphoreType.DMA((2,)),
        ],
        compiler_params=pltpu.CompilerParams(
            collective_id=0, has_side_effects=True, vmem_limit_bytes=56 * 1024 * 1024
        ),
        cost_estimate=pl.CostEstimate(
            flops=20 * slots * slots * channels,
            bytes_accessed=16 * slots * channels,
            transcendentals=slots * channels,
        ),
        name="monarch",
    )(
        owner.reshape(1, rows),
        middle_blocks.transpose(1, 2, 0).reshape(owners * owners, short),
        gate_gain.reshape(1, channels),
        gate_bias.reshape(1, channels),
        first_blocks,
        last_blocks,
        kernel,
        cotangent,
        rows_in,
    )
    grad_rows, grad_middle, grad_last, grad_kernel = pl.pallas_call(
        settle,
        out_shape=tuple(jax.ShapeDtypeStruct(held.shape, held.dtype) for held in results),
        in_specs=[anywhere] * 4,
        out_specs=[anywhere] * 4,
        scratch_shapes=[pltpu.VMEM(held.shape, held.dtype) for held in results]
        + [pltpu.SemaphoreType.DMA((16,)), pltpu.SemaphoreType.DMA((16,))],
        compiler_params=pltpu.CompilerParams(vmem_limit_bytes=56 * 1024 * 1024),
        name="settle",
    )(*results)
    grad_middle = grad_middle.reshape(owners // 2, owners, short).transpose(2, 0, 1)
    return (grad_rows, grad_middle, grad_last, grad_kernel)


def solution(mesh):
    placed = (
        P(("seqo", "seqi"), "width"),
        P(("seqo", "seqi"), None),
        P(("seqo", "seqi"), None, None),
        P(("seqo", "seqi"), None, None),
        P(("seqo", "seqi"), None, None),
        P(None, ("seqo", "seqi"), "width"),
        P("width"),
        P("width"),
        P(("seqo", "seqi"), "width"),
    )
    return jax.shard_map(
        per_device,
        mesh=mesh,
        in_specs=placed,
        out_specs=(
            P(("seqo", "seqi"), "width"),
            P(("seqo", "seqi"), "width", None),
            P(("seqo", "seqi"), "width", None),
            P(None, ("seqo", "seqi"), "width"),
        ),
        check_vma=False,
    )
```

```python
import functools
import jax
import jax.numpy as jnp
from jax import lax
from jax.experimental import pallas as pl
from jax.experimental.pallas import tpu as pltpu
from jax.sharding import PartitionSpec as P

CHUNKS = 4
MESH = pl.DeviceIdType.MESH


def deliver(buffer, owners):
    by_owner = buffer.reshape(owners, buffer.shape[0] // owners, buffer.shape[1])
    arrived = lax.all_to_all(by_owner, ("seqo", "seqi"), split_axis=0, concat_axis=0, tiled=True)
    return arrived.reshape(buffer.shape)


def regroup(blocks):
    arrived = lax.all_to_all(blocks, ("seqo", "seqi"), split_axis=1, concat_axis=1, tiled=True)
    return arrived


def per_device_plain(
    rows_in,
    owner,
    first_blocks,
    middle_blocks,
    last_blocks,
    kernel,
    gate_gain,
    gate_bias,
    cotangent,
):
    outer_count = lax.axis_size("seqo")
    owners = outer_count * lax.axis_size("seqi")
    channels = rows_in.shape[1]
    slots = cotangent.shape[0]
    capacity = slots // owners
    count_a = first_blocks.shape[0]
    block_size = first_blocks.shape[1]
    narrow = block_size // owners
    outer_len = middle_blocks.shape[1]
    target = owner[:, 0]
    matches = (target[:, None] == jnp.arange(owners, dtype=jnp.int32)[None, :]).astype(jnp.int32)
    order_rank = jnp.sum(matches * jnp.cumsum(matches, axis=0), axis=1) - 1
    slot_index = target * capacity + order_rank
    outbox = jnp.zeros((slots, channels), jnp.bfloat16).at[slot_index].set(rows_in)
    seq_in = deliver(outbox, owners).reshape(count_a, block_size, channels)
    gate_open = jax.nn.sigmoid(seq_in.astype(jnp.float32) * gate_gain + gate_bias)
    upstream = cotangent.reshape(count_a, block_size, channels).astype(jnp.float32)
    grad_mixed = (upstream * gate_open).astype(jnp.bfloat16)
    grad_weighted = jnp.einsum(
        "aij,aic->ajc", last_blocks, grad_mixed, preferred_element_type=jnp.float32
    ).astype(jnp.bfloat16)
    grad_wrows = grad_weighted.reshape(count_a, owners, narrow, channels)
    mixed_first = jnp.einsum(
        "aij,ajc->aic", first_blocks, seq_in, preferred_element_type=jnp.float32
    ).astype(jnp.bfloat16)
    first_rows = mixed_first.reshape(count_a, owners, narrow, channels)
    columns_in = regroup(first_rows)
    middle_view = middle_blocks.reshape(narrow, owners, count_a, owners, count_a)
    mixed_middle = jnp.einsum(
        "btmsl,lsbc->mtbc", middle_view, columns_in, preferred_element_type=jnp.float32
    )
    kernel_view = jnp.swapaxes(kernel.reshape(owners, count_a, narrow, channels), 0, 1).astype(
        jnp.float32
    )
    weighted_cols = (mixed_middle * kernel_view).astype(jnp.bfloat16)
    weighted = regroup(weighted_cols).reshape(count_a, block_size, channels)
    grad_cols = regroup(grad_wrows)
    grad_cols_f = grad_cols.astype(jnp.float32)
    grad_kern_view = (grad_cols_f * mixed_middle).astype(jnp.bfloat16)
    grad_kernel = jnp.swapaxes(grad_kern_view, 0, 1).reshape(outer_len, narrow, channels)
    grad_mid_in = (grad_cols_f * kernel_view).astype(jnp.bfloat16)
    part_middle = jnp.einsum(
        "mtbc,lsbc->btmsl", grad_mid_in, columns_in, preferred_element_type=jnp.float32
    )
    part_middle = part_middle.reshape(narrow, outer_len, outer_len)
    grad_first_cols = jnp.einsum(
        "btmsl,mtbc->lsbc", middle_view, grad_mid_in, preferred_element_type=jnp.float32
    ).astype(jnp.bfloat16)
    grad_first_out = regroup(grad_first_cols).reshape(count_a, block_size, channels)
    mixed_last = jnp.einsum(
        "aij,ajc->aic", last_blocks, weighted, preferred_element_type=jnp.float32
    )
    part_last = jnp.einsum("aic,ajc->aij", grad_mixed, weighted, preferred_element_type=jnp.float32)
    grad_seq = jnp.einsum(
        "aij,aic->ajc", first_blocks, grad_first_out, preferred_element_type=jnp.float32
    )
    grad_seq = grad_seq + upstream * mixed_last * gate_open * (1.0 - gate_open) * gate_gain
    returned = deliver(grad_seq.astype(jnp.bfloat16).reshape(slots, channels), owners)
    grad_rows = returned[slot_index]
    grad_middle, grad_last = (
        lax.psum_scatter(
            part_middle.astype(jnp.bfloat16), "width", scatter_dimension=1, tiled=True
        ).astype(jnp.float32),
        lax.psum_scatter(
            part_last.astype(jnp.bfloat16), "width", scatter_dimension=1, tiled=True
        ).astype(jnp.float32),
    )
    return (grad_rows, grad_middle, grad_last, grad_kernel)


def dot(a, b, contract):
    return lax.dot_general(
        a, b, (((contract[0],), (contract[1],)), ((), ())), preferred_element_type=jnp.float32
    )


def iota(shape, axis):
    return lax.broadcasted_iota(jnp.int32, shape, axis)


def fused(
    n_outer,
    n_inner,
    owner_ref,
    middle_ref,
    gain_ref,
    bias_ref,
    first_hbm,
    last_hbm,
    kernel_hbm,
    cot_hbm,
    rows_hbm,
    grad_rows_hbm,
    grad_middle_ref,
    grad_last_hbm,
    grad_kernel_hbm,
    grad_rows_ref,
    grad_last_ref,
    grad_kernel_ref,
    first_ref,
    last_ref,
    kernel_ref,
    cot_ref,
    rows_ref,
    onehot_ref,
    mid_ref,
    mixed_ref,
    factor_ref,
    part_last_ref,
    part_mid_ref,
    send_last,
    recv_last,
    send_mid,
    recv_mid,
    send_buf,
    recv_buf,
    load_sem,
    store_sem,
    rows_sem,
    send_sem,
    recv_sem,
    peer_send,
    peer_recv,
):
    owners = n_outer * n_inner
    wide = lax.axis_index("width")
    outer = lax.axis_index("seqo")
    inner = lax.axis_index("seqi")
    me = outer * n_inner + inner
    _, chunks, _, short, width = send_buf.shape
    slots = owners * short
    rows = rows_ref.shape[0]

    def partner(turn):
        to_outer = lax.rem(outer + turn // n_inner + 1, n_outer)
        to_inner = lax.rem(inner + lax.rem(turn, n_inner) + 1, n_inner)
        return to_outer, to_inner

    loads = [
        pltpu.make_async_copy(source, target, load_sem.at[at])
        for at, (source, target) in enumerate(
            (
                (first_hbm, first_ref),
                (last_hbm, last_ref),
                (kernel_hbm, kernel_ref),
                (cot_hbm, cot_ref),
                (rows_hbm, rows_ref),
            )
        )
    ]
    loads[4].start()

    barrier = pltpu.get_barrier_semaphore()

    @pl.loop(0, owners - 1)
    def _(turn):
        to_outer, to_inner = partner(turn)
        pl.semaphore_signal(
            barrier, inc=1, device_id=(wide, to_outer, to_inner), device_id_type=MESH
        )

    pl.semaphore_signal(barrier, inc=1, device_id=(1 - wide, outer, inner), device_id_type=MESH)

    def columns(chunk):
        return pl.ds(pl.multiple_of(chunk * width, width), width)

    def exchange(phase, chunk, values):
        blocks = values.astype(jnp.bfloat16).reshape(owners, short, width)
        send_buf[phase, chunk] = blocks
        recv_buf[phase, chunk, me] = send_buf[phase, chunk, me]

        @pl.loop(0, owners - 1)
        def _(turn):
            to_outer, to_inner = partner(turn)
            to = to_outer * n_inner + to_inner
            pltpu.make_async_remote_copy(
                src_ref=send_buf.at[phase, chunk, to],
                dst_ref=recv_buf.at[phase, chunk, me],
                send_sem=send_sem.at[phase, chunk],
                recv_sem=recv_sem.at[phase, chunk],
                device_id=(wide, to_outer, to_inner),
                device_id_type=MESH,
            ).start()

    def arrived(phase, chunk):
        part = recv_buf.at[phase, chunk, pl.ds(0, owners - 1)]
        pltpu.make_async_copy(part, part, recv_sem.at[phase, chunk]).wait()
        return recv_buf[phase, chunk].reshape(slots, width)

    target = owner_ref[...]
    matches = (target == iota((owners, rows), 0)).astype(jnp.float32)
    upper = (iota((rows, rows), 0) <= iota((rows, rows), 1)).astype(jnp.bfloat16)
    counts = dot(matches.astype(jnp.bfloat16), upper, (1, 0))
    rank = jnp.sum(matches * counts, axis=0, keepdims=True) - 1.0
    slot = target.astype(jnp.float32) * float(short) + rank
    onehot_ref[...] = (slot == iota((slots, rows), 0).astype(jnp.float32)).astype(jnp.bfloat16)

    for load in loads[:4]:
        load.start()
    loads[4].wait()
    pl.semaphore_wait(barrier, owners)

    def scatter_rows(chunk):
        exchange(0, chunk, dot(onehot_ref[...], rows_ref[:, columns(chunk)], (1, 0)))

    scatter_rows(0)
    scatter_rows(1)

    same_position = iota((slots, slots), 0) % short == iota((slots, slots), 1) % short
    pairs = owners * owners
    same_outer = (iota((pairs, slots), 0) % owners == iota((pairs, slots), 1) // short).astype(
        jnp.float32
    )
    spread = (iota((short, slots), 0) == iota((short, slots), 1) % short).astype(jnp.bfloat16)
    by_pair = (dot(middle_ref[...], spread, (1, 0)) * same_outer).astype(jnp.bfloat16)
    lift = (iota((slots, pairs), 0) // short == iota((slots, pairs), 1) // owners).astype(jnp.bfloat16)
    dense = dot(lift, by_pair, (1, 0))
    mid_ref[...] = jnp.where(same_position, dense, 0.0).astype(jnp.bfloat16)
    part_last_ref[...] = jnp.zeros_like(part_last_ref)
    part_mid_ref[...] = jnp.zeros_like(part_mid_ref)
    for load in loads[:4]:
        load.wait()

    def mix_first(chunk):
        seq = arrived(0, chunk)
        exchange(1, chunk, dot(first_ref[0], seq, (1, 0)))
        gain = gain_ref[:, columns(chunk)]
        gate = jax.nn.sigmoid(seq.astype(jnp.float32) * gain + bias_ref[:, columns(chunk)])
        upstream = cot_ref[:, columns(chunk)].astype(jnp.float32)
        mixed = (upstream * gate).astype(jnp.bfloat16)
        mixed_ref[:, columns(chunk)] = mixed
        exchange(2, chunk, dot(last_ref[0], mixed, (0, 0)))
        factor_ref[:, columns(chunk)] = upstream * gate * (1.0 - gate) * gain

    def mix_middle(chunk):
        first_cols = arrived(1, chunk)
        middle = dot(mid_ref[...], first_cols, (1, 0))
        taps = kernel_ref[:, :, columns(chunk)].reshape(slots, width).astype(jnp.float32)
        exchange(3, chunk, middle * taps)
        grad_cols = arrived(2, chunk).astype(jnp.float32)
        grad_mid_in = (grad_cols * taps).astype(jnp.bfloat16)
        exchange(4, chunk, dot(mid_ref[...], grad_mid_in, (0, 0)))
        grad_kernel_ref[:, :, columns(chunk)] = (
            (grad_cols * middle).astype(jnp.bfloat16).reshape(owners, short, width)
        )
        part_mid_ref[...] += dot(grad_mid_in, first_cols, (1, 1))

    def mix_last(chunk):
        weighted = arrived(3, chunk)
        local = dot(last_ref[0], weighted, (1, 0)) * factor_ref[:, columns(chunk)]
        exchange(5, chunk, dot(first_ref[0], arrived(4, chunk), (0, 0)) + local)
        part_last_ref[...] += dot(mixed_ref[:, columns(chunk)], weighted, (1, 1))

    @pl.loop(1, chunks + 3)
    def _(step):
        for lag, stage in enumerate((scatter_rows, mix_first, mix_middle, mix_last)):
            chunk = step - lag

            @pl.when((chunk >= (0 if lag else 2)) & (chunk < chunks))
            def _():
                stage(chunk)

    store_kernel = pltpu.make_async_copy(grad_kernel_ref, grad_kernel_hbm, store_sem.at[0])
    store_kernel.start()

    half = slots // 2
    send_last[...] = part_last_ref[...].astype(jnp.bfloat16).reshape(2, half, slots)
    diagonal = jnp.where(same_position, part_mid_ref[...], 0.0).astype(jnp.bfloat16)
    down = (iota((pairs, slots), 0) // owners == iota((pairs, slots), 1) // short).astype(jnp.bfloat16)
    gathered = (dot(down, diagonal, (1, 0)) * same_outer).astype(jnp.bfloat16)
    send_mid[...] = (
        dot(gathered, spread, (1, 1)).astype(jnp.bfloat16).reshape(2, pairs // 2, short)
    )
    peers = [
        pltpu.make_async_remote_copy(
            src_ref=source.at[1 - wide],
            dst_ref=landing,
            send_sem=peer_send.at[at],
            recv_sem=peer_recv.at[at],
            device_id=(1 - wide, outer, inner),
            device_id_type=MESH,
        )
        for at, (source, landing) in enumerate(((send_last, recv_last), (send_mid, recv_mid)))
    ]
    for copy in peers:
        copy.start()

    def store_rows(chunk):
        return pltpu.make_async_copy(
            grad_rows_ref.at[:, columns(chunk)],
            grad_rows_hbm.at[:, columns(chunk)],
            rows_sem.at[chunk],
        )

    def gather_rows(chunk):
        returned = arrived(5, chunk)
        grad_rows_ref[:, columns(chunk)] = dot(onehot_ref[...], returned, (0, 0)).astype(
            jnp.bfloat16
        )
        store_rows(chunk).start()

    @pl.loop(0, chunks - 1)
    def _(chunk):
        gather_rows(chunk)

    for copy in peers:
        copy.wait()
    grad_last_ref[0] = send_last[wide].astype(jnp.float32) + recv_last[...].astype(jnp.float32)
    store_last = pltpu.make_async_copy(grad_last_ref, grad_last_hbm, store_sem.at[1])
    store_last.start()
    grad_middle_ref[...] = send_mid[wide].astype(jnp.float32) + recv_mid[...].astype(jnp.float32)
    gather_rows(chunks - 1)

    @pl.loop(0, send_buf.shape[0])
    def _(phase):
        @pl.loop(0, chunks)
        def _(chunk):
            part = send_buf.at[phase, chunk, pl.ds(0, owners - 1)]
            pltpu.make_async_copy(part, part, send_sem.at[phase, chunk]).wait()

    @pl.loop(0, chunks)
    def _(chunk):
        store_rows(chunk).wait()

    store_kernel.wait()
    store_last.wait()


def settle(*refs):
    count = (len(refs) - 2) // 3
    sources, targets, held = refs[:count], refs[count : 2 * count], refs[2 * count : 3 * count]
    load_sem, store_sem = refs[3 * count :]
    loads, stores = [], []
    for at in range(count):
        pieces = 1 if sources[at].shape[0] == 1 else 4
        size = sources[at].shape[0] // pieces
        for piece in range(pieces):
            span, turn = pl.ds(piece * size, size), len(loads)
            here = held[at].at[span]
            loads.append(
                pltpu.make_async_copy(sources[at].at[span], here, load_sem.at[turn])
            )
            stores.append(
                pltpu.make_async_copy(here, targets[at].at[span], store_sem.at[turn])
            )
    for load in loads:
        load.start()
    for load, store in zip(loads, stores):
        load.wait()
        store.start()
    for store in stores:
        store.wait()


def per_device(
    rows_in,
    owner,
    first_blocks,
    middle_blocks,
    last_blocks,
    kernel,
    gate_gain,
    gate_bias,
    cotangent,
):
    n_outer, n_inner = lax.axis_size("seqo"), lax.axis_size("seqi")
    owners = n_outer * n_inner
    rows, channels = rows_in.shape
    slots = cotangent.shape[0]
    short = slots // owners
    if lax.axis_size("width") != 2 or short % 16 or first_blocks.shape[0] != 1:
        return per_device_plain(
            rows_in,
            owner,
            first_blocks,
            middle_blocks,
            last_blocks,
            kernel,
            gate_gain,
            gate_bias,
            cotangent,
        )
    width = channels // CHUNKS
    f32, bf16 = jnp.float32, jnp.bfloat16
    in_vmem = pl.BlockSpec(memory_space=pltpu.VMEM)
    anywhere = pl.BlockSpec(memory_space=pl.ANY)
    results = pl.pallas_call(
        functools.partial(fused, n_outer, n_inner),
        out_shape=(
            jax.ShapeDtypeStruct((rows, channels), bf16),
            jax.ShapeDtypeStruct((owners * owners // 2, short), f32),
            jax.ShapeDtypeStruct((1, slots // 2, slots), f32),
            jax.ShapeDtypeStruct(kernel.shape, bf16),
        ),
        in_specs=[in_vmem] * 4 + [anywhere] * 5,
        out_specs=[anywhere, in_vmem, anywhere, anywhere],
        scratch_shapes=[
            pltpu.VMEM((rows, channels), bf16),
            pltpu.VMEM((1, slots // 2, slots), f32),
            pltpu.VMEM(kernel.shape, bf16),
            pltpu.VMEM(first_blocks.shape, bf16),
            pltpu.VMEM(last_blocks.shape, bf16),
            pltpu.VMEM(kernel.shape, bf16),
            pltpu.VMEM(cotangent.shape, bf16),
            pltpu.VMEM(rows_in.shape, bf16),
            pltpu.VMEM((slots, rows), bf16),
            pltpu.VMEM((slots, slots), bf16),
            pltpu.VMEM((slots, channels), bf16),
            pltpu.VMEM((slots, channels), f32),
            pltpu.VMEM((slots, slots), f32),
            pltpu.VMEM((slots, slots), f32),
            pltpu.VMEM((2, slots // 2, slots), bf16),
            pltpu.VMEM((slots // 2, slots), bf16),
            pltpu.VMEM((2, owners * owners // 2, short), bf16),
            pltpu.VMEM((owners * owners // 2, short), bf16),
            pltpu.VMEM((6, CHUNKS, owners, short, width), bf16),
            pltpu.VMEM((6, CHUNKS, owners, short, width), bf16),
            pltpu.SemaphoreType.DMA((5,)),
            pltpu.SemaphoreType.DMA((2,)),
            pltpu.SemaphoreType.DMA((CHUNKS,)),
            pltpu.SemaphoreType.DMA((6, CHUNKS)),
            pltpu.SemaphoreType.DMA((6, CHUNKS)),
            pltpu.SemaphoreType.DMA((2,)),
            pltpu.SemaphoreType.DMA((2,)),
        ],
        compiler_params=pltpu.CompilerParams(
            collective_id=0, has_side_effects=True, vmem_limit_bytes=56 * 1024 * 1024
        ),
        cost_estimate=pl.CostEstimate(
            flops=20 * slots * slots * channels,
            bytes_accessed=16 * slots * channels,
            transcendentals=slots * channels,
        ),
        name="monarch",
    )(
        owner.reshape(1, rows),
        middle_blocks.transpose(1, 2, 0).reshape(owners * owners, short),
        gate_gain.reshape(1, channels),
        gate_bias.reshape(1, channels),
        first_blocks,
        last_blocks,
        kernel,
        cotangent,
        rows_in,
    )
    grad_rows, grad_middle, grad_last, grad_kernel = pl.pallas_call(
        settle,
        out_shape=tuple(jax.ShapeDtypeStruct(held.shape, held.dtype) for held in results),
        in_specs=[anywhere] * 4,
        out_specs=[anywhere] * 4,
        scratch_shapes=[pltpu.VMEM(held.shape, held.dtype) for held in results]
        + [pltpu.SemaphoreType.DMA((16,)), pltpu.SemaphoreType.DMA((16,))],
        compiler_params=pltpu.CompilerParams(vmem_limit_bytes=56 * 1024 * 1024),
        name="settle",
    )(*results)
    grad_middle = grad_middle.reshape(owners // 2, owners, short).transpose(2, 0, 1)
    return (grad_rows, grad_middle, grad_last, grad_kernel)


def solution(mesh):
    placed = (
        P(("seqo", "seqi"), "width"),
        P(("seqo", "seqi"), None),
        P(("seqo", "seqi"), None, None),
        P(("seqo", "seqi"), None, None),
        P(("seqo", "seqi"), None, None),
        P(None, ("seqo", "seqi"), "width"),
        P("width"),
        P("width"),
        P(("seqo", "seqi"), "width"),
    )
    return jax.shard_map(
        per_device,
        mesh=mesh,
        in_specs=placed,
        out_specs=(
            P(("seqo", "seqi"), "width"),
            P(("seqo", "seqi"), "width", None),
            P(("seqo", "seqi"), "width", None),
            P(None, ("seqo", "seqi"), "width"),
        ),
        check_vma=False,
    )
```
